32 devices in a mesh: chan: 8 (over y, x, core), tmpl: 4 (over z).
Axes of the slice: x: 2, y: 2, z: 4, core: 2. Of those that a mesh axis runs over, the one named last changes fastest.
Arguments:
- samples: bfloat16 [128, 384], P('chan'), may hold values from -200 to 200, as said below
- templates: bfloat16 [256, 16, 128], P('tmpl'), may hold values from -0.375 to 0.375
- start_chan: int32 [256], P('tmpl'), may hold values from 0 to 16, as said below
- chan_shift: int32 [128], P('chan'), may hold values from 0 to 128, as said below
- params: float32 [256, 16], P('tmpl'), may hold values from -4 to 4
Outputs:
- posterior: float32 [16, 128, 128], P(None, 'chan')
- evidence: float32 [128, 128], P('chan')
The draws below stay inside these ranges and needn't reach their ends.
Inputs may be any that keep to these rules, and one draw needn't show every extreme that they name: `samples`: each channel's record carries an amplitude of its own. `start_chan`: both ends reached in every draw. `chan_shift`: both ends reached in every draw.
All inputs are finite; a program needn't handle non-finite values.
Results may differ from the reference program's by a relative error of at most 0.00125.
Values may be sent and summed in bfloat16 or wider, within the bound.
A program may use at most 128 MiB of HBM per device.

```python
import jax
import jax.numpy as jnp
from jax import lax

T_POS = 128
TEMPLATES = 256
TCH = 16
TL = 128
PARAMS = 16
REACH = 16
SHIFT_MAX = 128
CHANNELS = 128
SAMPLES = 384
N_TMPL = 4


def draw_samples(key, part):
    key_base, key_amp = jax.random.split(key, 2)
    shape = (CHANNELS, SAMPLES)
    base = jax.random.truncated_normal(key_base, -4.0, 4.0, shape, jnp.float32)
    amp = jnp.exp(jax.random.uniform(key_amp, (CHANNELS, 1), jnp.float32, jnp.log(0.5), jnp.log(3.0)))
    return (base * amp).astype(jnp.bfloat16)


def draw_start_chan(key, part):
    top = 2 * REACH - TCH
    values = jax.random.randint(jax.random.fold_in(key, 11), (TEMPLATES,), 0, top + 1)
    return values.at[0].set(0).at[1].set(top).astype(jnp.int32)


def draw_chan_shift(key, part):
    values = jax.random.randint(jax.random.fold_in(key, 23), (CHANNELS,), 0, SHIFT_MAX + 1)
    return values.at[0].set(SHIFT_MAX).at[1].set(0).astype(jnp.int32)


def levels(rng, shape, cuts, smallest, largest):
    def one(dim, blocks):
        heights = jax.random.uniform(jax.random.fold_in(jax.random.fold_in(rng, 6), dim), (blocks,), jnp.float32, smallest / len(cuts), largest / len(cuts))
        return jnp.repeat(jnp.exp(heights), shape[dim] // blocks).reshape((-1,) + (1,) * (len(shape) - dim - 1))

    loudness = one(*cuts[0])
    for cut in cuts[1:]:
        loudness = loudness * one(*cut)
    return loudness


def centred(key, extent, deviation, reach, cuts=(), kind=jnp.bfloat16):
    result = deviation * jax.random.normal(key, extent, jnp.float32)
    if cuts:
        result = result * levels(key, extent, cuts, -0.22, 0.18)
    return jnp.clip(result, -reach, reach).astype(kind)


def setup_inputs(seed: int = 0) -> dict:
    splits = jax.random.split(jax.random.key(seed), 6)
    return {
        "samples": draw_samples(jax.random.fold_in(splits[5], 71), 0),
        "templates": centred(splits[1], (TEMPLATES, TCH, TL), (TCH * TL // 9) ** -0.5, 0.375, ((0, 4),)),
        "start_chan": draw_start_chan(jax.random.fold_in(splits[5], 71), 0),
        "chan_shift": draw_chan_shift(jax.random.fold_in(splits[5], 71), 0),
        "params": centred(splits[4], (TEMPLATES, PARAMS), 1.0, 4.0, ((0, 4),), jnp.float32),
    }


def shifted_rows(samples, chan_shift):
    return jax.vmap(lambda row, s: lax.dynamic_slice_in_dim(row, s.astype(jnp.int32), T_POS + TL))(samples, chan_shift)


def make_patches(padded):
    return jnp.stack([padded[:, l:l + T_POS] for l in range(TL)], axis=-1).reshape(-1, TL)


def block_scores(patches, templates, start_chan, rows_out):
    rows_in = patches.shape[0] // T_POS
    count = templates.shape[0]
    flat = templates.reshape(count * TCH, TL)
    plane = lax.dot_general(flat, patches, (((1,), (1,)), ((), ())), preferred_element_type=jnp.float32)
    plane = plane.reshape(count, TCH, rows_in, T_POS)
    offsets = (start_chan.astype(jnp.int32)[:, None] + jnp.arange(TCH, dtype=jnp.int32)[None, :]).astype(jnp.int32)
    pick_one = lambda r, s: lax.dynamic_slice_in_dim(r, s, rows_out, 0)
    picked = jax.vmap(jax.vmap(pick_one))(plane, offsets)
    return jnp.sum(picked, axis=1)


def local_state(scores, params):
    count, rows, width = scores.shape
    top = jnp.max(scores, axis=0)
    weights = jnp.exp(scores - top[None])
    total = jnp.sum(weights, axis=0)
    numer = lax.dot_general(params, weights.reshape(count, rows * width), (((0,), (0,)), ((), ())), precision=lax.Precision.HIGHEST, preferred_element_type=jnp.float32)
    return top, total, numer.reshape(PARAMS, rows, width)


def combine(first, second):
    top = jnp.maximum(first[0], second[0])
    scale_a = jnp.exp(first[0] - top)
    scale_b = jnp.exp(second[0] - top)
    return (top, first[1] * scale_a + second[1] * scale_b, first[2] * scale_a[None] + second[2] * scale_b[None])


def reference(samples, templates, start_chan, chan_shift, params):
    aligned = shifted_rows(samples, chan_shift)
    padded = jnp.pad(aligned, ((REACH, REACH), (0, 0)))
    patches = make_patches(padded)
    per_block = TEMPLATES // N_TMPL
    tblocks = templates.reshape(N_TMPL, per_block, TCH, TL)
    sblocks = start_chan.reshape(N_TMPL, per_block)
    pblocks = params.reshape(N_TMPL, per_block, PARAMS)

    def one_block(items):
        scores = block_scores(patches, items[0], items[1], CHANNELS)
        return local_state(scores, items[2])

    tops, totals, numers = lax.map(one_block, (tblocks, sblocks, pblocks))
    state = (tops[0], totals[0], numers[0])
    for b in range(1, N_TMPL):
        state = combine(state, (tops[b], totals[b], numers[b]))
    top, total, numer = state
    return numer / total[None], top + jnp.log(total)
```

```python
import functools

import jax
import jax.numpy as jnp
from jax import lax
from jax.experimental import pallas as pl
from jax.experimental.pallas import tpu as pltpu
from jax.sharding import PartitionSpec as P

T_POS = 128
TCH = 16
TL = 128
PARAMS = 16
REACH = 16
WIN = 2 * REACH
GROUP = 8
STEPS = 40
MESH = pl.DeviceIdType.MESH
F32, BF16 = jnp.float32, jnp.bfloat16


def column(row, n):
    wide = jnp.broadcast_to(row.astype(F32), (n, n))
    eye = lax.broadcasted_iota(jnp.int32, (n, n), 0) == lax.broadcasted_iota(jnp.int32, (n, n), 1)
    return jnp.sum(jnp.where(eye, wide, 0.0), axis=1, keepdims=True).astype(jnp.int32)


def build_filters(count, tmpl_ref, start_ref, tf, wp):
    tf[...] = tmpl_ref[...].astype(F32)
    start = column(start_ref[...], count)
    zero = jnp.zeros((count, (GROUP - 1) * TL), BF16)
    wp[:, : (GROUP - 1) * TL] = zero
    wp[:, (GROUP - 1 + WIN) * TL :] = jnp.zeros((count, GROUP * TL), BF16)
    step = 16
    for k0 in range(0, count, step):
        shift = jnp.broadcast_to(start[k0 : k0 + step], (step, TL))
        rows = [tf[pl.ds(k0 * TCH + j, step, stride=TCH), :] for j in range(TCH)]
        nothing = jnp.zeros((step, TL), F32)
        for bit in (1, 2, 4, 8, 16):
            on = (shift & bit) != 0
            size = min(WIN, len(rows) + bit)
            rows = [
                jnp.where(
                    on,
                    rows[r - bit] if r >= bit else nothing,
                    rows[r] if r < len(rows) else nothing,
                )
                for r in range(size)
            ]
        for r in range(WIN):
            wp[k0 : k0 + step, (GROUP - 1 + r) * TL : (GROUP + r) * TL] = rows[r].astype(BF16)


def build_hankel(block, first, e, h2):
    n = block.shape[0]
    for s in range(8):
        moved = block if s == 0 else pltpu.roll(block, 256 - s, 1)
        e[pl.ds(first * 8 + s, n, stride=8), :] = moved[:, :128]
        e[pl.ds((48 + first) * 8 + s, n, stride=8), :] = moved[:, 128:]
    lo = e[first * 8 : (first + n) * 8, :]
    hi = e[(48 + first) * 8 : (48 + first + n) * 8, :]
    both = jnp.concatenate([lo, hi], axis=1)

    def part(a):
        moved = both if a == 0 else pltpu.roll(both, 256 - 8 * a, 1)
        return moved[:, :128].reshape(n, 8, 128)

    for a in range(0, 16, 2):
        tile = jnp.concatenate([part(a), part(a + 1)], axis=1).astype(BF16)
        top = min(first + n, STEPS)
        if top > first:
            h2[first:top, 8 * a : 8 * a + 16, :128] = tile[: top - first]
        low = max(first, 8)
        h2[low - 8 : first + n - 8, 8 * a : 8 * a + 16, 128:] = tile[low - first :]


def kernel(
    nchan, nz, count,
    samples_ref, tmpl_ref, start_ref, shift_ref, params_ref,
    out_ref, ev_ref,
    al, halo, tf, wp, e, h2, comb, recv, gath,
    halo_send, halo_recv, rs_send, rs_recv, ag_send, ag_recv,
):
    cx, me = lax.axis_index("chan"), lax.axis_index("tmpl")
    q = 16 // nz
    has_left, has_right = cx > 0, cx < nchan - 1

    barrier = pltpu.get_barrier_semaphore()

    @pl.when(has_left)
    def _():
        pl.semaphore_signal(barrier, inc=1, device_id={"chan": cx - 1}, device_id_type=MESH)

    @pl.when(has_right)
    def _():
        pl.semaphore_signal(barrier, inc=1, device_id={"chan": cx + 1}, device_id_type=MESH)

    for d in range(1, nz):
        pl.semaphore_signal(
            barrier, inc=1, device_id={"tmpl": lax.rem(me + d, nz)}, device_id_type=MESH
        )

    x = samples_ref[...].astype(F32)
    shift = column(shift_ref[...], 16)
    for bit in (1, 2, 4, 8, 16, 32, 64, 128):
        on = (jnp.broadcast_to(shift, x.shape) & bit) != 0
        x = jnp.where(on, pltpu.roll(x, x.shape[1] - bit, 1), x)
    mine = x[:, : T_POS + TL]
    al[...] = mine.astype(BF16)

    pl.semaphore_wait(
        barrier, nz - 1 + has_left.astype(jnp.int32) + has_right.astype(jnp.int32)
    )

    def to_left():
        return pltpu.make_async_remote_copy(
            src_ref=al, dst_ref=halo.at[1], send_sem=halo_send.at[0], recv_sem=halo_recv.at[1],
            device_id={"chan": cx - 1}, device_id_type=MESH)

    def to_right():
        return pltpu.make_async_remote_copy(
            src_ref=al, dst_ref=halo.at[0], send_sem=halo_send.at[1], recv_sem=halo_recv.at[0],
            device_id={"chan": cx + 1}, device_id_type=MESH)

    @pl.when(has_left)
    def _():
        to_left().start()

    @pl.when(has_right)
    def _():
        to_right().start()

    build_filters(count, tmpl_ref, start_ref, tf, wp)
    build_hankel(mine, 16, e, h2)

    p = params_ref[...]
    p_hi = p.astype(BF16)
    p_lo = p - p_hi.astype(F32)
    below = (lax.broadcasted_iota(jnp.int32, (16, count), 0) == 0).astype(F32)
    pt_hi = jnp.concatenate([p_hi.astype(F32), below], axis=0).astype(BF16)
    pt_lo = jnp.concatenate([p_lo, jnp.zeros((16, count), F32)], axis=0).astype(BF16)

    @pl.when(has_left)
    def _():
        to_right().wait_recv()

    @pl.when(jnp.logical_not(has_left))
    def _():
        halo[0] = jnp.zeros((16, 256), BF16)

    @pl.when(has_right)
    def _():
        to_left().wait_recv()

    @pl.when(jnp.logical_not(has_right))
    def _():
        halo[1] = jnp.zeros((16, 256), BF16)

    build_hankel(halo[0].astype(F32), 0, e, h2)
    build_hankel(halo[1].astype(F32), 32, e, h2)

    lhs = jnp.concatenate(
        [wp[:, (GROUP - 1 - g) * TL : (GROUP - 1 - g + STEPS) * TL] for g in range(GROUP)], axis=0
    )
    scores = jnp.dot(lhs, h2[...].reshape(STEPS * TL, 256), preferred_element_type=F32)

    comb[:, q * 16 :, :] = jnp.zeros((nz, 8, 128), F32)

    def to_owner(z):
        slot = lax.rem(z - me + nz, nz)
        return pltpu.make_async_remote_copy(
            src_ref=comb.at[z], dst_ref=recv.at[slot], send_sem=rs_send.at[z],
            recv_sem=rs_recv.at[slot], device_id={"tmpl": z}, device_id_type=MESH)

    for g in range(GROUP):
        s = scores[g * count : (g + 1) * count]
        top = jnp.max(s, axis=0, keepdims=True)
        w = jnp.exp(s - top)
        w_hi = w.astype(BF16)
        w_lo = (w - w_hi.astype(F32)).astype(BF16)
        res = (
            jnp.dot(pt_hi, w_hi, preferred_element_type=F32)
            + jnp.dot(pt_hi, w_lo, preferred_element_type=F32)
            + jnp.dot(pt_lo, w_hi, preferred_element_type=F32)
        )
        total = res[PARAMS : PARAMS + 1]
        post = res[:PARAMS] / total
        ev = top + jnp.log(total)
        for half in range(2):
            i = 2 * g + half
            z, at = i // q, i % q
            comb[z, at * 16 : at * 16 + 16, :] = post[:, half * 128 : half * 128 + 128]
            comb[z, q * 16 + at : q * 16 + at + 1, :] = ev[:, half * 128 : half * 128 + 128]
            if at == q - 1:

                @pl.when(me != z)
                def _():
                    to_owner(z).start()

    for d in range(1, nz):
        pltpu.make_async_remote_copy(
            src_ref=comb.at[d], dst_ref=recv.at[d], send_sem=rs_send.at[d],
            recv_sem=rs_recv.at[d], device_id={"tmpl": lax.rem(me + d, nz)}, device_id_type=MESH
        ).wait_recv()

    evs = [comb[me, q * 16 :, :]] + [recv[d, q * 16 :, :] for d in range(1, nz)]
    top = functools.reduce(jnp.maximum, evs)
    parts = [jnp.exp(v - top) for v in evs]
    total = functools.reduce(jnp.add, parts)
    gath[me, q * 16 :, :] = top + jnp.log(total)
    inv = 1.0 / total
    shares = [v * inv for v in parts]
    for at in range(q):
        rows = slice(at * 16, at * 16 + 16)
        acc = shares[0][at : at + 1] * comb[me, rows, :]
        for d in range(1, nz):
            acc = acc + shares[d][at : at + 1] * recv[d, rows, :]
        gath[me, rows, :] = acc

    def to_peer(d):
        return pltpu.make_async_remote_copy(
            src_ref=gath.at[me], dst_ref=gath.at[me], send_sem=ag_send.at[d],
            recv_sem=ag_recv.at[me], device_id={"tmpl": lax.rem(me + d, nz)}, device_id_type=MESH)

    for d in range(1, nz):
        to_peer(d).start()
    for d in range(1, nz):
        z = lax.rem(me + d, nz)
        pltpu.make_async_remote_copy(
            src_ref=gath.at[z], dst_ref=gath.at[z], send_sem=ag_send.at[d],
            recv_sem=ag_recv.at[z], device_id={"tmpl": z}, device_id_type=MESH
        ).wait_recv()

    for i in range(16):
        c = 8 * (i % 2) + i // 2
        z, at = i // q, i % q
        out_ref[pl.ds(c, PARAMS, stride=16), :] = gath[z, at * 16 : at * 16 + 16, :]
        ev_ref[c : c + 1, :] = gath[z, q * 16 + at : q * 16 + at + 1, :]

    @pl.when(has_left)
    def _():
        to_left().wait_send()

    @pl.when(has_right)
    def _():
        to_right().wait_send()

    for z in range(nz):

        @pl.when(me != z)
        def _():
            to_owner(z).wait_send()

    for d in range(1, nz):
        to_peer(d).wait_send()


def solution(mesh):
    nchan, nz = mesh.shape["chan"], mesh.shape["tmpl"]

    def body(samples, templates, start_chan, chan_shift, params):
        rows, count = samples.shape[0], templates.shape[0]
        assert rows == 16 and 16 % nz == 0
        piece = 16 // nz * 16 + 8
        vmem = pl.BlockSpec(memory_space=pltpu.VMEM)
        dma = pltpu.SemaphoreType.DMA
        post, ev = pl.pallas_call(
            functools.partial(kernel, nchan, nz, count),
            out_shape=(
                jax.ShapeDtypeStruct((PARAMS * rows, T_POS), F32),
                jax.ShapeDtypeStruct((rows, T_POS), F32),
            ),
            in_specs=[vmem] * 5,
            out_specs=(vmem, vmem),
            scratch_shapes=[
                pltpu.VMEM((16, 256), BF16),
                pltpu.VMEM((2, 16, 256), BF16),
                pltpu.VMEM((count * TCH, TL), F32),
                pltpu.VMEM((count, (2 * GROUP - 1 + WIN) * TL), BF16),
                pltpu.VMEM((2 * 48 * 8, 128), F32),
                pltpu.VMEM((STEPS, TL, 256), BF16),
                pltpu.VMEM((nz, piece, 128), F32),
                pltpu.VMEM((nz, piece, 128), F32),
                pltpu.VMEM((nz, piece, 128), F32),
                dma((2,)),
                dma((2,)),
                dma((nz,)),
                dma((nz,)),
                dma((nz,)),
                dma((nz,)),
            ],
            compiler_params=pltpu.CompilerParams(
                collective_id=0, has_side_effects=True, vmem_limit_bytes=40 * 1024 * 1024
            ),
        )(
            samples,
            templates.reshape(count * TCH, TL),
            start_chan.reshape(1, count),
            chan_shift.reshape(1, rows),
            params.T,
        )
        return post.reshape(PARAMS, rows, T_POS), ev

    placed = (P("chan", None), P("tmpl", None, None), P("tmpl"), P("chan"), P("tmpl", None))
    return jax.shard_map(
        body,
        mesh=mesh,
        in_specs=placed,
        out_specs=(P(None, "chan", None), P("chan", None)),
        check_vma=False,
    )
```

```python
import functools

import jax
import jax.numpy as jnp
from jax import lax
from jax.experimental import pallas as pl
from jax.experimental.pallas import tpu as pltpu
from jax.sharding import PartitionSpec as P

T_POS = 128
TCH = 16
TL = 128
PARAMS = 16
REACH = 16
WIN = 2 * REACH
GROUP = 8
STEPS = 40
PARAM_MAX = 4.0
VMEM_BYTES = 60 * 1024 * 1024
CODE_MAX = 32767.0
MESH = pl.DeviceIdType.MESH
F32, BF16 = jnp.float32, jnp.bfloat16


def column(row, n):
    wide = jnp.broadcast_to(row.astype(F32), (n, n))
    eye = lax.broadcasted_iota(jnp.int32, (n, n), 0) == lax.broadcasted_iota(jnp.int32, (n, n), 1)
    return jnp.sum(jnp.where(eye, wide, 0.0), axis=1, keepdims=True).astype(jnp.int32)


def build_filters(count, tmpl_ref, start_ref, tf, wp):
    tf[...] = tmpl_ref[...].astype(F32)
    start = column(start_ref[...], count)
    zero = jnp.zeros((count, (GROUP - 1) * TL), BF16)
    wp[:, : (GROUP - 1) * TL] = zero
    wp[:, (GROUP - 1 + WIN) * TL :] = jnp.zeros((count, GROUP * TL), BF16)
    step = 16
    for k0 in range(0, count, step):
        shift = jnp.broadcast_to(start[k0 : k0 + step], (step, TL))
        rows = [tf[pl.ds(k0 * TCH + j, step, stride=TCH), :] for j in range(TCH)]
        nothing = jnp.zeros((step, TL), F32)
        for bit in (1, 2, 4, 8, 16):
            on = (shift & bit) != 0
            size = min(WIN, len(rows) + bit)
            rows = [
                jnp.where(
                    on,
                    rows[r - bit] if r >= bit else nothing,
                    rows[r] if r < len(rows) else nothing,
                )
                for r in range(size)
            ]
        for r in range(WIN):
            wp[k0 : k0 + step, (GROUP - 1 + r) * TL : (GROUP + r) * TL] = rows[r].astype(BF16)


def build_hankel(block, first, e, h2):
    n = block.shape[0]
    for s in range(8):
        moved = block if s == 0 else pltpu.roll(block, 256 - s, 1)
        e[pl.ds(first * 8 + s, n, stride=8), :] = moved[:, :128]
        e[pl.ds((48 + first) * 8 + s, n, stride=8), :] = moved[:, 128:]
    lo = e[first * 8 : (first + n) * 8, :]
    hi = e[(48 + first) * 8 : (48 + first + n) * 8, :]
    both = jnp.concatenate([lo, hi], axis=1)

    def part(a):
        moved = both if a == 0 else pltpu.roll(both, 256 - 8 * a, 1)
        return moved[:, :128].reshape(n, 8, 128)

    for a in range(0, 16, 2):
        tile = jnp.concatenate([part(a), part(a + 1)], axis=1).astype(BF16)
        top = min(first + n, STEPS)
        if top > first:
            h2[first:top, 8 * a : 8 * a + 16, :128] = tile[: top - first]
        low = max(first, 8)
        h2[low - 8 : first + n - 8, 8 * a : 8 * a + 16, 128:] = tile[low - first :]


def encode(x):
    m = jnp.clip(jnp.abs(x) * (1.0 / PARAM_MAX), 1e-30, 1.0)
    y = jnp.exp2(0.125 * jnp.log2(m)) * CODE_MAX
    return jnp.round(jnp.where(x < 0, -y, y)).astype(jnp.int16)


def decode(code):
    f = code.astype(F32)
    y = jnp.abs(f) * (1.0 / CODE_MAX)
    y = y * y
    y = y * y
    y = y * y * PARAM_MAX
    return jnp.where(f < 0, -y, y)


def kernel(
    nchan, nz, count,
    samples_hbm, tmpl_hbm, start_hbm, shift_hbm, params_hbm,
    gath, gev,
    samples_ref, tmpl_ref, start_ref, shift_ref, params_ref,
    al, halo, tf, wp, e, h2, comb, cev, recv, rev, fin, fev,
    in_sem, keep_sem, halo_send, halo_recv, rs_send, rs_recv, ag_send, ag_recv,
):
    cx, me = lax.axis_index("chan"), lax.axis_index("tmpl")
    q = 16 // nz
    has_left, has_right = cx > 0, cx < nchan - 1

    barrier = pltpu.get_barrier_semaphore()

    @pl.when(has_left)
    def _():
        pl.semaphore_signal(barrier, inc=1, device_id={"chan": cx - 1}, device_id_type=MESH)

    @pl.when(has_right)
    def _():
        pl.semaphore_signal(barrier, inc=1, device_id={"chan": cx + 1}, device_id_type=MESH)

    for d in range(1, nz):
        pl.semaphore_signal(
            barrier, inc=1, device_id={"tmpl": lax.rem(me + d, nz)}, device_id_type=MESH
        )

    loads = [
        pltpu.make_async_copy(src, dst, in_sem.at[i])
        for i, (src, dst) in enumerate(
            (
                (shift_hbm, shift_ref),
                (samples_hbm, samples_ref),
                (start_hbm, start_ref),
                (tmpl_hbm, tmpl_ref),
                (params_hbm, params_ref),
            )
        )
    ]
    for load in loads:
        load.start()

    loads[0].wait()
    loads[1].wait()
    x = samples_ref[...].astype(F32)
    shift = column(shift_ref[...], 16)
    for bit in (1, 2, 4, 8, 16, 32, 64, 128):
        on = (jnp.broadcast_to(shift, x.shape) & bit) != 0
        x = jnp.where(on, pltpu.roll(x, x.shape[1] - bit, 1), x)
    mine = x[:, : T_POS + TL]
    al[...] = mine.astype(BF16)

    pl.semaphore_wait(
        barrier, nz - 1 + has_left.astype(jnp.int32) + has_right.astype(jnp.int32)
    )

    def to_left():
        return pltpu.make_async_remote_copy(
            src_ref=al, dst_ref=halo.at[1], send_sem=halo_send.at[0], recv_sem=halo_recv.at[1],
            device_id={"chan": cx - 1}, device_id_type=MESH)

    def to_right():
        return pltpu.make_async_remote_copy(
            src_ref=al, dst_ref=halo.at[0], send_sem=halo_send.at[1], recv_sem=halo_recv.at[0],
            device_id={"chan": cx + 1}, device_id_type=MESH)

    @pl.when(has_left)
    def _():
        to_left().start()

    @pl.when(has_right)
    def _():
        to_right().start()

    loads[2].wait()
    loads[3].wait()
    loads[4].wait()
    build_filters(count, tmpl_ref, start_ref, tf, wp)
    build_hankel(mine, 16, e, h2)

    p = params_ref[...]
    p_hi = p.astype(BF16)
    p_lo = p - p_hi.astype(F32)
    below = (lax.broadcasted_iota(jnp.int32, (16, count), 0) == 0).astype(F32)
    pt_hi = jnp.concatenate([p_hi.astype(F32), below], axis=0).astype(BF16)
    pt_lo = jnp.concatenate([p_lo, jnp.zeros((16, count), F32)], axis=0).astype(BF16)

    @pl.when(has_left)
    def _():
        to_right().wait_recv()

    @pl.when(jnp.logical_not(has_left))
    def _():
        halo[0] = jnp.zeros((16, 256), BF16)

    @pl.when(has_right)
    def _():
        to_left().wait_recv()

    @pl.when(jnp.logical_not(has_right))
    def _():
        halo[1] = jnp.zeros((16, 256), BF16)

    build_hankel(halo[0].astype(F32), 0, e, h2)
    build_hankel(halo[1].astype(F32), 32, e, h2)

    lhs = jnp.concatenate(
        [wp[:, (GROUP - 1 - g) * TL : (GROUP - 1 - g + STEPS) * TL] for g in range(GROUP)], axis=0
    )
    scores = jnp.dot(lhs, h2[...].reshape(STEPS * TL, 256), preferred_element_type=F32)

    cev[...] = jnp.zeros((nz, 8, 128), F32)

    def to_owner(z):
        slot = lax.rem(z - me + nz, nz)
        return [
            pltpu.make_async_remote_copy(
                src_ref=src.at[z], dst_ref=dst.at[slot], send_sem=rs_send.at[n, z],
                recv_sem=rs_recv.at[n, slot], device_id={"tmpl": z}, device_id_type=MESH)
            for n, (src, dst) in enumerate(((cev, rev), (comb, recv)))
        ]

    for g in range(GROUP):
        s = scores[g * count : (g + 1) * count]
        top = jnp.max(s, axis=0, keepdims=True)
        w = jnp.exp(s - top)
        w_hi = w.astype(BF16)
        w_lo = (w - w_hi.astype(F32)).astype(BF16)
        res = (
            jnp.dot(pt_hi, w_hi, preferred_element_type=F32)
            + jnp.dot(pt_hi, w_lo, preferred_element_type=F32)
            + jnp.dot(pt_lo, w_hi, preferred_element_type=F32)
        )
        total = res[PARAMS : PARAMS + 1]
        code = encode(res[:PARAMS] / total)
        ev = top + jnp.log(total)
        for half in range(2):
            i = 2 * g + half
            z, at = i // q, i % q
            comb[z, at * 16 : at * 16 + 16, :] = code[:, half * 128 : half * 128 + 128]
            cev[z, at : at + 1, :] = ev[:, half * 128 : half * 128 + 128]
            if at == q - 1:

                @pl.when(me != z)
                def _():
                    for copy in to_owner(z):
                        copy.start()

    for d in range(1, nz):
        for n, (src, dst) in enumerate(((cev, rev), (comb, recv))):
            pltpu.make_async_remote_copy(
                src_ref=src.at[d], dst_ref=dst.at[d], send_sem=rs_send.at[n, d],
                recv_sem=rs_recv.at[n, d], device_id={"tmpl": lax.rem(me + d, nz)},
                device_id_type=MESH).wait_recv()

    evs = [cev[me]] + [rev[d] for d in range(1, nz)]
    top = functools.reduce(jnp.maximum, evs)
    parts = [jnp.exp(v - top) for v in evs]
    total = functools.reduce(jnp.add, parts)
    fev[...] = top + jnp.log(total)
    inv = 1.0 / total
    shares = [v * inv for v in parts]
    for at in range(q):
        rows = slice(at * 16, at * 16 + 16)
        acc = shares[0][at : at + 1] * decode(comb[me, rows, :])
        for d in range(1, nz):
            acc = acc + shares[d][at : at + 1] * decode(recv[d, rows, :])
        fin[rows, :] = encode(acc)

    def to_peer(d):
        return [
            pltpu.make_async_remote_copy(
                src_ref=src, dst_ref=ref.at[me], send_sem=ag_send.at[n, d],
                recv_sem=ag_recv.at[n, me], device_id={"tmpl": lax.rem(me + d, nz)},
                device_id_type=MESH)
            for n, (src, ref) in enumerate(((fev, gev), (fin, gath)))
        ]

    for d in range(1, nz):
        for copy in to_peer(d):
            copy.start()
    keeps = [
        pltpu.make_async_copy(fev, gev.at[me], keep_sem.at[0]),
        pltpu.make_async_copy(fin, gath.at[me], keep_sem.at[1]),
    ]
    for keep in keeps:
        keep.start()
    for d in range(1, nz):
        z = lax.rem(me + d, nz)
        for n, (src, ref) in enumerate(((fev, gev), (fin, gath))):
            pltpu.make_async_remote_copy(
                src_ref=src, dst_ref=ref.at[z], send_sem=ag_send.at[n, d],
                recv_sem=ag_recv.at[n, z], device_id={"tmpl": z}, device_id_type=MESH
            ).wait_recv()
    for keep in keeps:
        keep.wait()

    @pl.when(has_left)
    def _():
        to_left().wait_send()

    @pl.when(has_right)
    def _():
        to_right().wait_send()

    for z in range(nz):

        @pl.when(me != z)
        def _():
            for copy in to_owner(z):
                copy.wait_send()

    for d in range(1, nz):
        for copy in to_peer(d):
            copy.wait_send()


def unpack(nz, gath_hbm, gev_hbm, out_hbm, ev_hbm, gath, gev, out_ref, ev_ref, in_sem, sem):
    q = 16 // nz
    load = pltpu.make_async_copy(gev_hbm, gev, in_sem.at[nz])
    loads = [pltpu.make_async_copy(gath_hbm.at[z], gath.at[z], in_sem.at[z]) for z in range(nz)]
    load.start()
    for copy in loads:
        copy.start()
    load.wait()
    for i in range(16):
        if i % q == 0:
            loads[i // q].wait()
        c = 8 * (i % 2) + i // 2
        z, at = i // q, i % q
        ev_ref[c : c + 1, :] = gev[z, at : at + 1, :]
        out_ref[pl.ds(c, PARAMS, stride=16), :] = decode(gath[z, at * 16 : at * 16 + 16, :])
    copies = [
        pltpu.make_async_copy(ev_ref, ev_hbm, sem.at[0]),
        pltpu.make_async_copy(out_ref, out_hbm, sem.at[1]),
    ]
    for copy in copies:
        copy.start()
    for copy in copies:
        copy.wait()


def solution(mesh):
    nchan, nz = mesh.shape["chan"], mesh.shape["tmpl"]

    def body(samples, templates, start_chan, chan_shift, params):
        rows, count = samples.shape[0], templates.shape[0]
        assert rows == 16 and 16 % nz == 0
        piece = 16 // nz * 16
        hbm = pl.BlockSpec(memory_space=pltpu.HBM)
        dma = pltpu.SemaphoreType.DMA
        codes = pltpu.VMEM((nz, piece, 128), jnp.int16)
        evs = pltpu.VMEM((nz, 8, 128), F32)
        gath, gev = pl.pallas_call(
            functools.partial(kernel, nchan, nz, count),
            out_shape=(
                jax.ShapeDtypeStruct((nz, piece, 128), jnp.int16),
                jax.ShapeDtypeStruct((nz, 8, 128), F32),
            ),
            in_specs=[hbm] * 5,
            out_specs=(hbm, hbm),
            scratch_shapes=[
                pltpu.VMEM(samples.shape, BF16),
                pltpu.VMEM((count * TCH, TL), BF16),
                pltpu.VMEM((1, count), jnp.int32),
                pltpu.VMEM((1, rows), jnp.int32),
                pltpu.VMEM((PARAMS, count), F32),
                pltpu.VMEM((16, 256), BF16),
                pltpu.VMEM((2, 16, 256), BF16),
                pltpu.VMEM((count * TCH, TL), F32),
                pltpu.VMEM((count, (2 * GROUP - 1 + WIN) * TL), BF16),
                pltpu.VMEM((2 * 48 * 8, 128), F32),
                pltpu.VMEM((STEPS, TL, 256), BF16),
                codes, evs, codes, evs,
                pltpu.VMEM((piece, 128), jnp.int16),
                pltpu.VMEM((8, 128), F32),
                dma((5,)),
                dma((2,)),
                dma((2,)),
                dma((2,)),
                dma((2, nz)),
                dma((2, nz)),
                dma((2, nz)),
                dma((2, nz)),
            ],
            compiler_params=pltpu.CompilerParams(
                collective_id=0, has_side_effects=True, vmem_limit_bytes=VMEM_BYTES
            ),
        )(
            samples,
            templates.reshape(count * TCH, TL),
            start_chan.reshape(1, count),
            chan_shift.reshape(1, rows),
            params.T,
        )
        post, ev = pl.pallas_call(
            functools.partial(unpack, nz),
            out_shape=(
                jax.ShapeDtypeStruct((PARAMS * rows, T_POS), F32),
                jax.ShapeDtypeStruct((rows, T_POS), F32),
            ),
            in_specs=[hbm, hbm],
            out_specs=(hbm, hbm),
            scratch_shapes=[
                codes, evs,
                pltpu.VMEM((PARAMS * rows, T_POS), F32),
                pltpu.VMEM((rows, T_POS), F32),
                dma((nz + 1,)),
                dma((2,)),
            ],
            compiler_params=pltpu.CompilerParams(vmem_limit_bytes=VMEM_BYTES),
        )(gath, gev)
        return post.reshape(PARAMS, rows, T_POS), ev

    placed = (P("chan", None), P("tmpl", None, None), P("tmpl"), P("chan"), P("tmpl", None))
    return jax.shard_map(
        body,
        mesh=mesh,
        in_specs=placed,
        out_specs=(P(None, "chan", None), P("chan", None)),
        check_vma=False,
    )
```

```python
import functools

import jax
import jax.numpy as jnp
from jax import lax
from jax.experimental import pallas as pl
from jax.experimental.pallas import tpu as pltpu
from jax.sharding import PartitionSpec as P

T_POS = 128
TCH = 16
TL = 128
PARAMS = 16
REACH = 16
WIN = 2 * REACH
GROUP = 8
STEPS = 40
PARAM_MAX = 4.0
VMEM_BYTES = 40 * 1024 * 1024
CODE_MAX = 32767.0
EV_STEP = 8.0
EV_FINE = 8191.0
MESH = pl.DeviceIdType.MESH
F32, BF16 = jnp.float32, jnp.bfloat16


def column(row, n):
    wide = jnp.broadcast_to(row.astype(F32), (n, n))
    eye = lax.broadcasted_iota(jnp.int32, (n, n), 0) == lax.broadcasted_iota(jnp.int32, (n, n), 1)
    return jnp.sum(jnp.where(eye, wide, 0.0), axis=1, keepdims=True).astype(jnp.int32)


def build_filters(count, tmpl_ref, start_ref, tf, wp):
    tf[...] = tmpl_ref[...].astype(F32)
    start = column(start_ref[...], count)
    zero = jnp.zeros((count, (GROUP - 1) * TL), BF16)
    wp[:, : (GROUP - 1) * TL] = zero
    wp[:, (GROUP - 1 + WIN) * TL :] = jnp.zeros((count, GROUP * TL), BF16)
    step = 16
    for k0 in range(0, count, step):
        shift = jnp.broadcast_to(start[k0 : k0 + step], (step, TL))
        rows = [tf[pl.ds(k0 * TCH + j, step, stride=TCH), :] for j in range(TCH)]
        nothing = jnp.zeros((step, TL), F32)
        for bit in (1, 2, 4, 8, 16):
            on = (shift & bit) != 0
            size = min(WIN, len(rows) + bit)
            rows = [
                jnp.where(
                    on,
                    rows[r - bit] if r >= bit else nothing,
                    rows[r] if r < len(rows) else nothing,
                )
                for r in range(size)
            ]
        for r in range(WIN):
            wp[k0 : k0 + step, (GROUP - 1 + r) * TL : (GROUP + r) * TL] = rows[r].astype(BF16)


def build_hankel(block, first, e, h2):
    n = block.shape[0]
    for s in range(8):
        moved = block if s == 0 else pltpu.roll(block, 256 - s, 1)
        e[pl.ds(first * 8 + s, n, stride=8), :] = moved[:, :128]
        e[pl.ds((48 + first) * 8 + s, n, stride=8), :] = moved[:, 128:]
    lo = e[first * 8 : (first + n) * 8, :]
    hi = e[(48 + first) * 8 : (48 + first + n) * 8, :]
    both = jnp.concatenate([lo, hi], axis=1)

    def part(a):
        moved = both if a == 0 else pltpu.roll(both, 256 - 8 * a, 1)
        return moved[:, :128].reshape(n, 8, 128)

    for a in range(0, 16, 2):
        tile = jnp.concatenate([part(a), part(a + 1)], axis=1).astype(BF16)
        top = min(first + n, STEPS)
        if top > first:
            h2[first:top, 8 * a : 8 * a + 16, :128] = tile[: top - first]
        low = max(first, 8)
        h2[low - 8 : first + n - 8, 8 * a : 8 * a + 16, 128:] = tile[low - first :]


def encode(x):
    m = jnp.clip(jnp.abs(x) * (1.0 / PARAM_MAX), 1e-30, 1.0)
    y = jnp.exp2(0.125 * jnp.log2(m)) * CODE_MAX
    return jnp.round(jnp.where(x < 0, -y, y)).astype(jnp.int16)


def decode(code):
    f = code.astype(F32)
    y = jnp.abs(f) * (1.0 / CODE_MAX)
    y = y * y
    y = y * y
    y = y * y * PARAM_MAX
    return jnp.where(f < 0, -y, y)


def encode_evidence(ev):
    coarse = jnp.round(ev * (1.0 / EV_STEP))
    fine = jnp.round((ev - coarse * EV_STEP) * EV_FINE)
    return jnp.concatenate([coarse, fine], axis=0).astype(jnp.int16)


def decode_evidence(code):
    f = code.astype(F32)
    return f[:8] * EV_STEP + f[8:] * (1.0 / EV_FINE)


def align(x, shift_row):
    shift = column(shift_row, x.shape[0])
    for bit in (1, 2, 4, 8, 16, 32, 64, 128):
        on = (jnp.broadcast_to(shift, x.shape) & bit) != 0
        x = jnp.where(on, pltpu.roll(x, x.shape[1] - bit, 1), x)
    return x[:, : T_POS + TL]


def kernel(
    nchan, nz, count,
    samples_hbm, tmpl_hbm, start_hbm, shift_hbm, params_hbm,
    gath,
    samples_ref, tmpl_ref, start_ref, shift_ref, params_ref,
    al, halo, tf, wp, e, h2, comb, cev, recv,
    in_sem, halo_send, halo_recv, rs_send, rs_recv, ag_send, ag_recv,
):
    cx, me = lax.axis_index("chan"), lax.axis_index("tmpl")
    q = 16 // nz
    has_left, has_right = cx > 0, cx < nchan - 1

    barrier = pltpu.get_barrier_semaphore()

    @pl.when(has_left)
    def _():
        pl.semaphore_signal(barrier, inc=1, device_id={"chan": cx - 1}, device_id_type=MESH)

    @pl.when(has_right)
    def _():
        pl.semaphore_signal(barrier, inc=1, device_id={"chan": cx + 1}, device_id_type=MESH)

    for d in range(1, nz):
        pl.semaphore_signal(
            barrier, inc=1, device_id={"tmpl": lax.rem(me + d, nz)}, device_id_type=MESH
        )

    loads = [
        pltpu.make_async_copy(src, dst, in_sem.at[i])
        for i, (src, dst) in enumerate(
            (
                (shift_hbm, shift_ref),
                (samples_hbm, samples_ref),
                (start_hbm, start_ref),
                (tmpl_hbm, tmpl_ref),
                (params_hbm, params_ref),
            )
        )
    ]
    for load in loads:
        load.start()

    loads[0].wait()
    loads[1].wait()
    mine = align(samples_ref[...].astype(F32), shift_ref[...])
    al[...] = mine.astype(BF16)

    pl.semaphore_wait(
        barrier, nz - 1 + has_left.astype(jnp.int32) + has_right.astype(jnp.int32)
    )

    def to_side(side):
        land = 1 - side
        return pltpu.make_async_remote_copy(
            src_ref=al, dst_ref=halo.at[land], send_sem=halo_send.at[side],
            recv_sem=halo_recv.at[land], device_id={"chan": cx + 2 * side - 1},
            device_id_type=MESH)

    def send_side(side):
        to_side(side).start()

    def got_from(side):
        to_side(1 - side).wait_recv()

    def none_from(side):
        halo[side] = jnp.zeros(halo.shape[1:], BF16)

    def sent_side(side):
        to_side(side).wait_send()

    pl.when(has_left)(lambda: send_side(0))
    pl.when(has_right)(lambda: send_side(1))

    loads[2].wait()
    loads[3].wait()
    loads[4].wait()
    build_filters(count, tmpl_ref, start_ref, tf, wp)
    build_hankel(mine, 16, e, h2)

    p = params_ref[...]
    p_hi = p.astype(BF16)
    p_lo = p - p_hi.astype(F32)
    below = (lax.broadcasted_iota(jnp.int32, (16, count), 0) == 0).astype(F32)
    pt_hi = jnp.concatenate([p_hi.astype(F32), below], axis=0).astype(BF16)
    pt_lo = jnp.concatenate([p_lo, jnp.zeros((16, count), F32)], axis=0).astype(BF16)

    pl.when(has_left)(lambda: got_from(0))
    pl.when(jnp.logical_not(has_left))(lambda: none_from(0))
    pl.when(has_right)(lambda: got_from(1))
    pl.when(jnp.logical_not(has_right))(lambda: none_from(1))

    build_hankel(halo[0].astype(F32), 0, e, h2)
    build_hankel(halo[1].astype(F32), 32, e, h2)

    lhs = jnp.concatenate(
        [wp[:, (GROUP - 1 - g) * TL : (GROUP - 1 - g + STEPS) * TL] for g in range(GROUP)], axis=0
    )
    scores = jnp.dot(lhs, h2[...].reshape(STEPS * TL, 256), preferred_element_type=F32)

    cev[...] = jnp.zeros((nz, 8, 128), F32)

    def to_owner(z):
        slot = lax.rem(z - me + nz, nz)
        return pltpu.make_async_remote_copy(
            src_ref=comb.at[z], dst_ref=recv.at[slot], send_sem=rs_send.at[z],
            recv_sem=rs_recv.at[slot], device_id={"tmpl": z}, device_id_type=MESH)

    for g in range(GROUP):
        s = scores[g * count : (g + 1) * count]
        top = jnp.max(s, axis=0, keepdims=True)
        w = jnp.exp(s - top)
        w_hi = w.astype(BF16)
        w_lo = (w - w_hi.astype(F32)).astype(BF16)
        res = (
            jnp.dot(pt_hi, w_hi, preferred_element_type=F32)
            + jnp.dot(pt_hi, w_lo, preferred_element_type=F32)
            + jnp.dot(pt_lo, w_hi, preferred_element_type=F32)
        )
        total = res[PARAMS : PARAMS + 1]
        code = encode(res[:PARAMS] / total)
        ev = top + jnp.log(total)
        for half in range(2):
            i = 2 * g + half
            z, at = i // q, i % q
            comb[z, at * 16 : at * 16 + 16, :] = code[:, half * 128 : half * 128 + 128]
            cev[z, at : at + 1, :] = ev[:, half * 128 : half * 128 + 128]
            if at == q - 1:
                comb[z, q * 16 :, :] = encode_evidence(cev[z])

                @pl.when(me != z)
                def _():
                    to_owner(z).start()

    for d in range(1, nz):
        pltpu.make_async_remote_copy(
            src_ref=comb.at[d], dst_ref=recv.at[d], send_sem=rs_send.at[d],
            recv_sem=rs_recv.at[d], device_id={"tmpl": lax.rem(me + d, nz)},
            device_id_type=MESH).wait_recv()

    evs = [cev[me]] + [decode_evidence(recv[d, q * 16 :, :]) for d in range(1, nz)]
    top = functools.reduce(jnp.maximum, evs)
    parts = [jnp.exp(v - top) for v in evs]
    total = functools.reduce(jnp.add, parts)
    gath[me, q * 16 :, :] = encode_evidence(top + jnp.log(total))
    inv = 1.0 / total
    shares = [v * inv for v in parts]
    for at in range(q):
        rows = slice(at * 16, at * 16 + 16)
        acc = shares[0][at : at + 1] * decode(comb[me, rows, :])
        for d in range(1, nz):
            acc = acc + shares[d][at : at + 1] * decode(recv[d, rows, :])
        gath[me, rows, :] = encode(acc)

    def to_peer(d):
        return pltpu.make_async_remote_copy(
            src_ref=gath.at[me], dst_ref=gath.at[me], send_sem=ag_send.at[d],
            recv_sem=ag_recv.at[me], device_id={"tmpl": lax.rem(me + d, nz)}, device_id_type=MESH)

    for d in range(1, nz):
        to_peer(d).start()

    pl.when(has_left)(lambda: sent_side(0))
    pl.when(has_right)(lambda: sent_side(1))
    for z in range(nz):

        @pl.when(me != z)
        def _():
            to_owner(z).wait_send()

    for d in range(1, nz):
        z = lax.rem(me + d, nz)
        pltpu.make_async_remote_copy(
            src_ref=gath.at[z], dst_ref=gath.at[z], send_sem=ag_send.at[d],
            recv_sem=ag_recv.at[z], device_id={"tmpl": z}, device_id_type=MESH).wait_recv()
    for d in range(1, nz):
        to_peer(d).wait_send()


def unpack(nz, gath, out_hbm, ev_hbm, out_ref, ev_ref, sem):
    q = 16 // nz
    for z in range(nz):
        ev = decode_evidence(gath[z, q * 16 :, :])
        for at in range(q):
            i = z * q + at
            c = 8 * (i % 2) + i // 2
            ev_ref[c : c + 1, :] = ev[at : at + 1]
            out_ref[pl.ds(c, PARAMS, stride=16), :] = decode(gath[z, at * 16 : at * 16 + 16, :])
    copies = [
        pltpu.make_async_copy(ev_ref, ev_hbm, sem.at[0]),
        pltpu.make_async_copy(out_ref, out_hbm, sem.at[1]),
    ]
    for copy in copies:
        copy.start()
    for copy in copies:
        copy.wait()


def solution(mesh):
    nchan, nz = mesh.shape["chan"], mesh.shape["tmpl"]

    def body(samples, templates, start_chan, chan_shift, params):
        rows, count = samples.shape[0], templates.shape[0]
        assert rows == 16 and 16 % nz == 0
        piece = 16 // nz * 16 + 16
        vmem = pl.BlockSpec(memory_space=pltpu.VMEM)
        hbm = pl.BlockSpec(memory_space=pltpu.HBM)
        dma = pltpu.SemaphoreType.DMA
        codes = pltpu.VMEM((nz, piece, 128), jnp.int16)
        evs = pltpu.VMEM((nz, 8, 128), F32)
        gath = pl.pallas_call(
            functools.partial(kernel, nchan, nz, count),
            out_shape=pltpu.VMEM((nz, piece, 128), jnp.int16),
            in_specs=[hbm] * 5,
            out_specs=vmem,
            scratch_shapes=[
                pltpu.VMEM(samples.shape, BF16),
                pltpu.VMEM((count * TCH, TL), BF16),
                pltpu.VMEM((1, count), jnp.int32),
                pltpu.VMEM((1, rows), jnp.int32),
                pltpu.VMEM((PARAMS, count), F32),
                pltpu.VMEM((16, 256), BF16),
                pltpu.VMEM((2, 16, 256), BF16),
                pltpu.VMEM((count * TCH, TL), F32),
                pltpu.VMEM((count, (2 * GROUP - 1 + WIN) * TL), BF16),
                pltpu.VMEM((2 * 48 * 8, 128), F32),
                pltpu.VMEM((STEPS, TL, 256), BF16),
                codes, evs, codes,
                dma((5,)),
                dma((2,)),
                dma((2,)),
                dma((nz,)),
                dma((nz,)),
                dma((nz,)),
                dma((nz,)),
            ],
            compiler_params=pltpu.CompilerParams(
                collective_id=0, has_side_effects=True, vmem_limit_bytes=VMEM_BYTES
            ),
        )(
            *(
                pltpu.with_memory_space_constraint(v, pltpu.HBM)
                for v in (
                    samples,
                    templates.reshape(count * TCH, TL),
                    start_chan.reshape(1, count),
                    chan_shift.reshape(1, rows),
                    params.T,
                )
            )
        )
        post, ev = pl.pallas_call(
            functools.partial(unpack, nz),
            out_shape=(
                jax.ShapeDtypeStruct((PARAMS * rows, T_POS), F32),
                jax.ShapeDtypeStruct((rows, T_POS), F32),
            ),
            in_specs=[vmem],
            out_specs=(hbm, hbm),
            scratch_shapes=[
                pltpu.VMEM((PARAMS * rows, T_POS), F32),
                pltpu.VMEM((rows, T_POS), F32),
                dma((2,)),
            ],
            compiler_params=pltpu.CompilerParams(vmem_limit_bytes=VMEM_BYTES),
        )(gath)
        return post.reshape(PARAMS, rows, T_POS), ev

    placed = (P("chan", None), P("tmpl", None, None), P("tmpl"), P("chan"), P("tmpl", None))
    return jax.shard_map(
        body,
        mesh=mesh,
        in_specs=placed,
        out_specs=(P(None, "chan", None), P("chan", None)),
        check_vma=False,
    )
```

```python
import functools

import jax
import jax.numpy as jnp
from jax import lax
from jax.experimental import pallas as pl
from jax.experimental.pallas import tpu as pltpu
from jax.sharding import PartitionSpec as P

T_POS = 128
TCH = 16
TL = 128
PARAMS = 16
REACH = 16
WIN = 2 * REACH
GROUP = 8
STEPS = 40
PARAM_MAX = 4.0
VMEM_BYTES = 40 * 1024 * 1024
CODE_MAX = 32767.0
EV_STEP = 8.0
EV_FINE = 8191.0
MESH = pl.DeviceIdType.MESH
F32, BF16 = jnp.float32, jnp.bfloat16


def column(row, n):
    wide = jnp.broadcast_to(row.astype(F32), (n, n))
    eye = lax.broadcasted_iota(jnp.int32, (n, n), 0) == lax.broadcasted_iota(jnp.int32, (n, n), 1)
    return jnp.sum(jnp.where(eye, wide, 0.0), axis=1, keepdims=True).astype(jnp.int32)


def build_filters(count, tmpl_ref, start_ref, tf, wp):
    tf[...] = tmpl_ref[...].astype(F32)
    start = column(start_ref[...], count)
    zero = jnp.zeros((count, (GROUP - 1) * TL), BF16)
    wp[:, : (GROUP - 1) * TL] = zero
    wp[:, (GROUP - 1 + WIN) * TL :] = jnp.zeros((count, GROUP * TL), BF16)
    step = 16
    for k0 in range(0, count, step):
        shift = jnp.broadcast_to(start[k0 : k0 + step], (step, TL))
        rows = [tf[pl.ds(k0 * TCH + j, step, stride=TCH), :] for j in range(TCH)]
        nothing = jnp.zeros((step, TL), F32)
        for bit in (1, 2, 4, 8, 16):
            on = (shift & bit) != 0
            size = min(WIN, len(rows) + bit)
            rows = [
                jnp.where(
                    on,
                    rows[r - bit] if r >= bit else nothing,
                    rows[r] if r < len(rows) else nothing,
                )
                for r in range(size)
            ]
        for r in range(WIN):
            wp[k0 : k0 + step, (GROUP - 1 + r) * TL : (GROUP + r) * TL] = rows[r].astype(BF16)


def build_hankel(block, first, e, h2):
    n = block.shape[0]
    for s in range(8):
        moved = block if s == 0 else pltpu.roll(block, 256 - s, 1)
        e[pl.ds(first * 8 + s, n, stride=8), :] = moved[:, :128]
        e[pl.ds((48 + first) * 8 + s, n, stride=8), :] = moved[:, 128:]
    lo = e[first * 8 : (first + n) * 8, :]
    hi = e[(48 + first) * 8 : (48 + first + n) * 8, :]
    both = jnp.concatenate([lo, hi], axis=1)

    def part(a):
        moved = both if a == 0 else pltpu.roll(both, 256 - 8 * a, 1)
        return moved[:, :128].reshape(n, 8, 128)

    for a in range(0, 16, 2):
        tile = jnp.concatenate([part(a), part(a + 1)], axis=1).astype(BF16)
        top = min(first + n, STEPS)
        if top > first:
            h2[first:top, 8 * a : 8 * a + 16, :128] = tile[: top - first]
        low = max(first, 8)
        h2[low - 8 : first + n - 8, 8 * a : 8 * a + 16, 128:] = tile[low - first :]


def encode(x):
    m = jnp.clip(jnp.abs(x) * (1.0 / PARAM_MAX), 1e-30, 1.0)
    y = jnp.exp2(0.125 * jnp.log2(m)) * CODE_MAX
    return jnp.round(jnp.where(x < 0, -y, y)).astype(jnp.int16)


def decode(code):
    f = code.astype(F32)
    y = jnp.abs(f) * (1.0 / CODE_MAX)
    y = y * y
    y = y * y
    y = y * y * PARAM_MAX
    return jnp.where(f < 0, -y, y)


def encode_evidence(ev):
    coarse = jnp.round(ev * (1.0 / EV_STEP))
    fine = jnp.round((ev - coarse * EV_STEP) * EV_FINE)
    return jnp.concatenate([coarse, fine], axis=0).astype(jnp.int16)


def decode_evidence(code):
    f = code.astype(F32)
    return f[:8] * EV_STEP + f[8:] * (1.0 / EV_FINE)


def align(x, shift_row):
    shift = column(shift_row, x.shape[0])
    for bit in (1, 2, 4, 8, 16, 32, 64, 128):
        on = (jnp.broadcast_to(shift, x.shape) & bit) != 0
        x = jnp.where(on, pltpu.roll(x, x.shape[1] - bit, 1), x)
    return x[:, : T_POS + TL]


def kernel(
    nchan, nz, count,
    samples_hbm, tmpl_hbm, start_hbm, shift_hbm, params_hbm,
    gath,
    samples_ref, tmpl_ref, start_ref, shift_ref, params_ref,
    al, halo, tf, wp, e, h2, comb, cev, recv,
    in_sem, halo_send, halo_recv, rs_send, rs_recv, ag_send, ag_recv,
):
    cx, me = lax.axis_index("chan"), lax.axis_index("tmpl")
    q = 16 // nz
    has_left, has_right = cx > 0, cx < nchan - 1

    barrier = pltpu.get_barrier_semaphore()

    @pl.when(has_left)
    def _():
        pl.semaphore_signal(barrier, inc=1, device_id={"chan": cx - 1}, device_id_type=MESH)

    @pl.when(has_right)
    def _():
        pl.semaphore_signal(barrier, inc=1, device_id={"chan": cx + 1}, device_id_type=MESH)

    for d in range(1, nz):
        pl.semaphore_signal(
            barrier, inc=1, device_id={"tmpl": lax.rem(me + d, nz)}, device_id_type=MESH
        )

    loads = [
        pltpu.make_async_copy(src, dst, in_sem.at[i])
        for i, (src, dst) in enumerate(
            (
                (shift_hbm, shift_ref),
                (samples_hbm, samples_ref),
                (start_hbm, start_ref),
                (tmpl_hbm, tmpl_ref),
                (params_hbm, params_ref),
            )
        )
    ]
    for load in loads:
        load.start()

    loads[0].wait()
    loads[1].wait()
    mine = align(samples_ref[...].astype(F32), shift_ref[...])
    al[...] = mine.astype(BF16)

    pl.semaphore_wait(
        barrier, nz - 1 + has_left.astype(jnp.int32) + has_right.astype(jnp.int32)
    )

    def to_side(side):
        land = 1 - side
        return pltpu.make_async_remote_copy(
            src_ref=al, dst_ref=halo.at[land], send_sem=halo_send.at[side],
            recv_sem=halo_recv.at[land], device_id={"chan": cx + 2 * side - 1},
            device_id_type=MESH)

    def send_side(side):
        to_side(side).start()

    def got_from(side):
        to_side(1 - side).wait_recv()

    def none_from(side):
        halo[side] = jnp.zeros(halo.shape[1:], BF16)

    def sent_side(side):
        to_side(side).wait_send()

    pl.when(has_left)(lambda: send_side(0))
    pl.when(has_right)(lambda: send_side(1))

    loads[2].wait()
    loads[3].wait()
    loads[4].wait()
    build_filters(count, tmpl_ref, start_ref, tf, wp)
    build_hankel(mine, 16, e, h2)

    p = params_ref[...]
    p_hi = p.astype(BF16)
    p_lo = p - p_hi.astype(F32)
    below = (lax.broadcasted_iota(jnp.int32, (16, count), 0) == 0).astype(F32)
    pt_hi = jnp.concatenate([p_hi.astype(F32), below], axis=0).astype(BF16)
    pt_lo = jnp.concatenate([p_lo, jnp.zeros((16, count), F32)], axis=0).astype(BF16)

    pl.when(has_left)(lambda: got_from(0))
    pl.when(jnp.logical_not(has_left))(lambda: none_from(0))

    build_hankel(halo[0].astype(F32), 0, e, h2)
    pl.when(has_right)(lambda: got_from(1))
    pl.when(jnp.logical_not(has_right))(lambda: none_from(1))
    build_hankel(halo[1].astype(F32), 32, e, h2)

    lhs = jnp.concatenate(
        [wp[:, (GROUP - 1 - g) * TL : (GROUP - 1 - g + STEPS) * TL] for g in range(GROUP)], axis=0
    )
    scores = jnp.dot(lhs, h2[...].reshape(STEPS * TL, 256), preferred_element_type=F32)

    cev[...] = jnp.zeros((nz, 8, 128), F32)

    def to_owner(z):
        slot = lax.rem(z - me + nz, nz)
        return pltpu.make_async_remote_copy(
            src_ref=comb.at[z], dst_ref=recv.at[slot], send_sem=rs_send.at[z],
            recv_sem=rs_recv.at[slot], device_id={"tmpl": z}, device_id_type=MESH)

    for g in range(GROUP):
        s = scores[g * count : (g + 1) * count]
        top = jnp.max(s, axis=0, keepdims=True)
        w = jnp.exp(s - top)
        w_hi = w.astype(BF16)
        w_lo = (w - w_hi.astype(F32)).astype(BF16)
        res = (
            jnp.dot(pt_hi, w_hi, preferred_element_type=F32)
            + jnp.dot(pt_hi, w_lo, preferred_element_type=F32)
            + jnp.dot(pt_lo, w_hi, preferred_element_type=F32)
        )
        total = res[PARAMS : PARAMS + 1]
        code = encode(res[:PARAMS] / total)
        ev = top + jnp.log(total)
        for half in range(2):
            i = 2 * g + half
            z, at = i // q, i % q
            comb[z, at * 16 : at * 16 + 16, :] = code[:, half * 128 : half * 128 + 128]
            cev[z, at : at + 1, :] = ev[:, half * 128 : half * 128 + 128]
            if at == q - 1:
                comb[z, q * 16 :, :] = encode_evidence(cev[z])

                @pl.when(me != z)
                def _():
                    to_owner(z).start()

    for d in range(1, nz):
        pltpu.make_async_remote_copy(
            src_ref=comb.at[d], dst_ref=recv.at[d], send_sem=rs_send.at[d],
            recv_sem=rs_recv.at[d], device_id={"tmpl": lax.rem(me + d, nz)},
            device_id_type=MESH).wait_recv()

    evs = [cev[me]] + [decode_evidence(recv[d, q * 16 :, :]) for d in range(1, nz)]
    top = functools.reduce(jnp.maximum, evs)
    parts = [jnp.exp(v - top) for v in evs]
    total = functools.reduce(jnp.add, parts)
    gath[me, q * 16 :, :] = encode_evidence(top + jnp.log(total))
    inv = 1.0 / total
    shares = [v * inv for v in parts]
    for at in range(q):
        rows = slice(at * 16, at * 16 + 16)
        acc = shares[0][at : at + 1] * decode(comb[me, rows, :])
        for d in range(1, nz):
            acc = acc + shares[d][at : at + 1] * decode(recv[d, rows, :])
        gath[me, rows, :] = encode(acc)

    def to_peer(d):
        return pltpu.make_async_remote_copy(
            src_ref=gath.at[me], dst_ref=gath.at[me], send_sem=ag_send.at[d],
            recv_sem=ag_recv.at[me], device_id={"tmpl": lax.rem(me + d, nz)}, device_id_type=MESH)

    for d in range(1, nz):
        to_peer(d).start()

    pl.when(has_left)(lambda: sent_side(0))
    pl.when(has_right)(lambda: sent_side(1))
    for z in range(nz):

        @pl.when(me != z)
        def _():
            to_owner(z).wait_send()

    for d in range(1, nz):
        z = lax.rem(me + d, nz)
        pltpu.make_async_remote_copy(
            src_ref=gath.at[z], dst_ref=gath.at[z], send_sem=ag_send.at[d],
            recv_sem=ag_recv.at[z], device_id={"tmpl": z}, device_id_type=MESH).wait_recv()
    for d in range(1, nz):
        to_peer(d).wait_send()


def unpack(nz, gath, out_hbm, ev_hbm, out_ref, ev_ref, sem):
    q = 16 // nz
    for z in range(nz):
        ev = decode_evidence(gath[z, q * 16 :, :])
        for at in range(q):
            i = z * q + at
            c = 8 * (i % 2) + i // 2
            ev_ref[c : c + 1, :] = ev[at : at + 1]
            out_ref[pl.ds(c, PARAMS, stride=16), :] = decode(gath[z, at * 16 : at * 16 + 16, :])
    copies = [
        pltpu.make_async_copy(ev_ref, ev_hbm, sem.at[0]),
        pltpu.make_async_copy(out_ref, out_hbm, sem.at[1]),
    ]
    for copy in copies:
        copy.start()
    for copy in copies:
        copy.wait()


def solution(mesh):
    nchan, nz = mesh.shape["chan"], mesh.shape["tmpl"]

    def body(samples, templates, start_chan, chan_shift, params):
        rows, count = samples.shape[0], templates.shape[0]
        assert rows == 16 and 16 % nz == 0
        piece = 16 // nz * 16 + 16
        vmem = pl.BlockSpec(memory_space=pltpu.VMEM)
        hbm = pl.BlockSpec(memory_space=pltpu.HBM)
        dma = pltpu.SemaphoreType.DMA
        codes = pltpu.VMEM((nz, piece, 128), jnp.int16)
        evs = pltpu.VMEM((nz, 8, 128), F32)
        gath = pl.pallas_call(
            functools.partial(kernel, nchan, nz, count),
            out_shape=pltpu.VMEM((nz, piece, 128), jnp.int16),
            in_specs=[hbm] * 5,
            out_specs=vmem,
            scratch_shapes=[
                pltpu.VMEM(samples.shape, BF16),
                pltpu.VMEM((count * TCH, TL), BF16),
                pltpu.VMEM((1, count), jnp.int32),
                pltpu.VMEM((1, rows), jnp.int32),
                pltpu.VMEM((PARAMS, count), F32),
                pltpu.VMEM((16, 256), BF16),
                pltpu.VMEM((2, 16, 256), BF16),
                pltpu.VMEM((count * TCH, TL), F32),
                pltpu.VMEM((count, (2 * GROUP - 1 + WIN) * TL), BF16),
                pltpu.VMEM((2 * 48 * 8, 128), F32),
                pltpu.VMEM((STEPS, TL, 256), BF16),
                codes, evs, codes,
                dma((5,)),
                dma((2,)),
                dma((2,)),
                dma((nz,)),
                dma((nz,)),
                dma((nz,)),
                dma((nz,)),
            ],
            compiler_params=pltpu.CompilerParams(
                collective_id=0, has_side_effects=True, vmem_limit_bytes=VMEM_BYTES
            ),
        )(
            *(
                pltpu.with_memory_space_constraint(v, pltpu.HBM)
                for v in (
                    samples,
                    templates.reshape(count * TCH, TL),
                    start_chan.reshape(1, count),
                    chan_shift.reshape(1, rows),
                    params.T,
                )
            )
        )
        post, ev = pl.pallas_call(
            functools.partial(unpack, nz),
            out_shape=(
                jax.ShapeDtypeStruct((PARAMS * rows, T_POS), F32),
                jax.ShapeDtypeStruct((rows, T_POS), F32),
            ),
            in_specs=[vmem],
            out_specs=(hbm, hbm),
            scratch_shapes=[
                pltpu.VMEM((PARAMS * rows, T_POS), F32),
                pltpu.VMEM((rows, T_POS), F32),
                dma((2,)),
            ],
            compiler_params=pltpu.CompilerParams(vmem_limit_bytes=VMEM_BYTES),
        )(gath)
        return post.reshape(PARAMS, rows, T_POS), ev

    placed = (P("chan", None), P("tmpl", None, None), P("tmpl"), P("chan"), P("tmpl", None))
    return jax.shard_map(
        body,
        mesh=mesh,
        in_specs=placed,
        out_specs=(P(None, "chan", None), P("chan", None)),
        check_vma=False,
    )
```
